32 devices in a mesh: groups: 2 (over x), feat: 8 (over z, y), tgt: 2 (over core).
Axes of the slice: x: 2, y: 2, z: 4, core: 2. Of those that a mesh axis runs over, the one named last changes fastest.
Arguments:
- inputs: float32 [1536, 2304], P(('groups', 'feat')), parts along dimension 0, may hold values from -6 to 6
- preacts: bfloat16 [1536, 16384], P('groups', 'feat'), parts along dimension 0, may hold values from -6 to 6
- cotangent: float32 [2, 1536, 2304], P('tgt', ('groups', 'feat')), parts along dimension 1, may hold values from -1.5 to 1.5
- w_enc: bfloat16 [2304, 16384], P(None, 'feat'), may hold values from -0.125 to 0.125
- w_dec: bfloat16 [2, 16384, 2304], P('tgt', 'feat'), may hold values from -0.046875 to 0.046875
Outputs:
- grad_dec: float32 [4, 16384, 2304], P(('groups', 'tgt'), 'feat'), parts along dimension 0
- grad_enc: float32 [4608, 16384], P(('groups', 'tgt'), 'feat'), parts along dimension 0
- grad_bias: float32 [32768], P(('groups', 'feat')), parts along dimension 0
- grad_inputs: float32 [1536, 2304], P(('groups', 'feat'), 'tgt'), parts along dimension 0
The draws below stay inside these ranges and needn't reach their ends.
There are 2 independent parts, one for each index of `groups`. The reference program is written for one: setup_inputs(seed, part) draws one part's arguments, and reference() takes and returns one part's arrays. A program takes and returns all parts, laid end to end along the dimension named above; an argument that names none is the same for every part. Nothing has to cross between parts.
All inputs are finite; a program needn't handle non-finite values.
Results may differ from the reference program's by a relative error of at most 0.005.
Values may be sent and summed in bfloat16 or wider, within the bound.
A program may use at most 128 MiB of HBM per device.

```python
import jax
import jax.numpy as jnp

D = 2304
F = 16384
TOK = 768
LAYERS = 2


def level_of(own_key, shape, pieces, smallest, top_value):
    def one(position, parts):
        steps = jax.random.uniform(jax.random.fold_in(jax.random.fold_in(own_key, 6), position), (parts,), jnp.float32, smallest / len(pieces), top_value / len(pieces))
        return jnp.repeat(jnp.exp(steps), shape[position] // parts).reshape((-1,) + (1,) * (len(shape) - position - 1))

    factor_of = one(*pieces[0])
    for cut in pieces[1:]:
        factor_of = factor_of * one(*cut)
    return factor_of


def noise(key, extent, deviation, bound, shards=(), held_as=jnp.bfloat16):
    level = level_of(key, extent, shards, -0.22, 0.18) if shards else 1.0
    drawn = jax.random.normal(key, extent, jnp.float32) * deviation * level
    return jnp.minimum(jnp.maximum(drawn, -bound), bound).astype(held_as)


def setup_inputs(seed: int = 0, part: int = 0) -> dict:
    streams_of = jax.random.split(jax.random.key(seed), 6)
    own_keys = jax.random.split(jax.random.fold_in(streams_of[5], part), 6)
    return {
        "inputs": noise(own_keys[0], (TOK, D), 1.0, 6.0, ((0, 8),), jnp.float32),
        "preacts": noise(own_keys[1], (TOK, F), 1.0, 6.0, ((1, 8),)),
        "cotangent": noise(own_keys[2], (LAYERS, TOK, D), 0.25, 1.5, ((0, 2), (1, 8)), jnp.float32),
        "w_enc": noise(streams_of[3], (D, F), D ** -0.5, 0.125, ((1, 8),)),
        "w_dec": noise(streams_of[4], (LAYERS, F, D), F ** -0.5, 0.046875, ((0, 2), (1, 8))),
    }


def reference(inputs, preacts, cotangent, w_enc, w_dec):
    active = jnp.maximum(preacts, 0).astype(jnp.bfloat16)
    back_rows = cotangent.astype(jnp.bfloat16)
    grads = []
    feat_grad = jnp.zeros((TOK, F), jnp.float32)
    for layer_idx in range(LAYERS):
        grads.append(jnp.dot(active.T, back_rows[layer_idx], preferred_element_type=jnp.float32))
        feat_grad = feat_grad + jnp.dot(back_rows[layer_idx], w_dec[layer_idx].T, preferred_element_type=jnp.float32)
    grad_dec = jnp.stack(grads)
    pre_grad = jnp.where(preacts > 0, feat_grad, jnp.zeros_like(feat_grad)).astype(jnp.bfloat16)
    input_rows = inputs.astype(jnp.bfloat16)
    grad_enc = jnp.dot(input_rows.T, pre_grad, preferred_element_type=jnp.float32)
    grad_bias = jnp.sum(pre_grad.astype(jnp.float32), axis=0)
    grad_inputs = jnp.dot(pre_grad, w_enc.T, preferred_element_type=jnp.float32)
    return (grad_dec, grad_enc, grad_bias, grad_inputs)
```

```python
import functools

import jax
import jax.numpy as jnp
from jax import lax
from jax.experimental import pallas as pl
from jax.experimental.pallas import tpu as pltpu
from jax.sharding import PartitionSpec as P

MESH = pl.DeviceIdType.MESH


def gather_kernel(n, cot_ref, all_ref, up_sem, down_sem, side_sem, recv_sem):
    deep = n // 2
    me = lax.axis_index("feat")
    z, y = me // 2, lax.rem(me, 2)
    mate = 2 * z + 1 - y

    def to(block, sem, target):
        return pltpu.make_async_remote_copy(
            src_ref=all_ref.at[block],
            dst_ref=all_ref.at[block],
            send_sem=sem,
            recv_sem=recv_sem.at[block],
            device_id={"feat": target},
            device_id_type=MESH,
        )

    all_ref[me] = cot_ref[...].astype(jnp.bfloat16)

    barrier = pltpu.get_barrier_semaphore()
    pl.semaphore_signal(barrier, inc=1, device_id={"feat": mate}, device_id_type=MESH)

    @pl.when(z + 1 < deep)
    def _():
        pl.semaphore_signal(barrier, inc=1, device_id={"feat": me + 2}, device_id_type=MESH)

    @pl.when(z > 0)
    def _():
        pl.semaphore_signal(barrier, inc=1, device_id={"feat": me - 2}, device_id_type=MESH)

    pl.semaphore_wait(barrier, 1 + jnp.where(z + 1 < deep, 1, 0) + jnp.where(z > 0, 1, 0))

    to(me, side_sem.at[z], mate).start()

    @pl.when(z + 1 < deep)
    def _():
        to(me, up_sem.at[z], me + 2).start()

    @pl.when(z > 0)
    def _():
        to(me, down_sem.at[z], me - 2).start()

    for step in range(1, deep):
        low, high = z - step, z + step

        @pl.when(low >= 0)
        def _():
            block = 2 * low + y
            to(block, side_sem.at[low], mate).wait_recv()

            @pl.when(z + 1 < deep)
            def _():
                to(block, up_sem.at[low], me + 2).start()

            to(block, side_sem.at[low], mate).start()

        @pl.when(high < deep)
        def _():
            block = 2 * high + y
            to(block, side_sem.at[high], mate).wait_recv()

            @pl.when(z > 0)
            def _():
                to(block, down_sem.at[high], me - 2).start()

            to(block, side_sem.at[high], mate).start()

    for row in range(deep):
        to(2 * row + 1 - y, side_sem.at[row], mate).wait_recv()
    for row in range(deep):
        block = 2 * row + y
        to(block, side_sem.at[row], mate).wait_send()

        @pl.when((row <= z) & (z + 1 < deep))
        def _():
            to(block, up_sem.at[row], mate).wait_send()

        @pl.when((row >= z) & (z > 0))
        def _():
            to(block, down_sem.at[row], mate).wait_send()


def gather(cot, n):
    tok, width = cot.shape
    deep = n // 2
    return pl.pallas_call(
        functools.partial(gather_kernel, n),
        out_shape=jax.ShapeDtypeStruct((n, tok, width), jnp.bfloat16),
        in_specs=[pl.BlockSpec(memory_space=pltpu.VMEM)],
        out_specs=pl.BlockSpec(memory_space=pltpu.VMEM),
        scratch_shapes=[
            pltpu.SemaphoreType.DMA((deep,)),
            pltpu.SemaphoreType.DMA((deep,)),
            pltpu.SemaphoreType.DMA((deep,)),
            pltpu.SemaphoreType.DMA((n,)),
        ],
        compiler_params=pltpu.CompilerParams(
            collective_id=0, has_side_effects=True, vmem_limit_bytes=24 * 1024 * 1024
        ),
        cost_estimate=pl.CostEstimate(
            flops=0, bytes_accessed=40 * n * tok * width, transcendentals=0
        ),
    )(cot)


def body(inputs, preacts, cotangent, w_enc, w_dec):
    n = lax.axis_size("feat")
    deep = n // 2
    tok = inputs.shape[0]
    f_loc = preacts.shape[1]
    me = lax.axis_index("feat")
    z, y = me // 2, lax.rem(me, 2)
    tgt_index = lax.axis_index("tgt")
    half_width = inputs.shape[1] // lax.axis_size("tgt")

    back_all = gather(cotangent[0], n)
    input_half = lax.dynamic_slice_in_dim(inputs, tgt_index * half_width, half_width, 1).astype(
        jnp.bfloat16
    )
    back_all, input_half = lax.optimization_barrier((back_all, input_half))
    input_all = lax.all_gather(input_half, "feat", axis=0, tiled=True)
    back_all = back_all.reshape(n * tok, -1)

    partial_value = lax.dot_general(
        back_all, w_dec[0], (((1,), (1,)), ((), ())), preferred_element_type=jnp.float32
    ).astype(jnp.bfloat16)
    other = lax.ppermute(partial_value, "tgt", [(0, 1), (1, 0)])
    summed = partial_value.astype(jnp.float32) + other.astype(jnp.float32)
    pre_grad = jnp.where(preacts > 0, summed, jnp.zeros_like(summed)).astype(jnp.bfloat16)
    grad_bias = jnp.sum(pre_grad.astype(jnp.float32), axis=0)

    enc_half = lax.dynamic_slice_in_dim(w_enc, tgt_index * half_width, half_width, 0)
    part = lax.dot_general(
        pre_grad, enc_half, (((1,), (1,)), ((), ())), preferred_element_type=jnp.float32
    ).astype(jnp.bfloat16)
    part = part.reshape(deep, 2, tok, half_width)
    theirs = lax.dynamic_index_in_dim(part, 1 - y, 1, keepdims=False)
    mine = lax.dynamic_index_in_dim(part, y, 1, keepdims=False)
    arrived = lax.ppermute(theirs, "feat", [(i, i ^ 1) for i in range(n)])

    active = jnp.maximum(preacts, 0)
    grad_dec = lax.dot_general(
        active, back_all, (((0,), (0,)), ((), ())), preferred_element_type=jnp.float32
    )[None]

    both = mine.astype(jnp.float32) + arrived.astype(jnp.float32)
    total = lax.dynamic_index_in_dim(both, z, 0, keepdims=False)
    sent = both.astype(jnp.bfloat16)
    for step in range(1, deep):
        block = lax.dynamic_index_in_dim(sent, lax.rem(z + step, deep), 0, keepdims=False)
        got = lax.ppermute(block, "feat", [(i, (i + 2 * step) % n) for i in range(n)])
        total = total + got.astype(jnp.float32)
    grad_enc = lax.dot_general(
        input_all, pre_grad, (((0,), (0,)), ((), ())), preferred_element_type=jnp.float32
    )
    return (grad_dec, grad_enc, grad_bias, total)


def solution(mesh):
    in_specs = (
        P(("groups", "feat"), None),
        P("groups", "feat"),
        P("tgt", ("groups", "feat"), None),
        P(None, "feat"),
        P("tgt", "feat", None),
    )
    out_specs = (
        P(("groups", "tgt"), "feat", None),
        P(("groups", "tgt"), "feat"),
        P(("groups", "feat")),
        P(("groups", "feat"), "tgt"),
    )
    return jax.shard_map(body, mesh=mesh, in_specs=in_specs, out_specs=out_specs, check_vma=False)
```

```python
import functools

import jax
import jax.numpy as jnp
from jax import lax
from jax.experimental import pallas as pl
from jax.experimental.pallas import tpu as pltpu
from jax.sharding import PartitionSpec as P

MESH = pl.DeviceIdType.MESH


def gather_kernel(n, cot_ref, all_ref, up_sem, down_sem, side_sem, recv_sem):
    deep = n // 2
    me = lax.axis_index("feat")
    z, y = me // 2, lax.rem(me, 2)
    mate = 2 * z + 1 - y

    def to(block, sem, target):
        return pltpu.make_async_remote_copy(
            src_ref=all_ref.at[block],
            dst_ref=all_ref.at[block],
            send_sem=sem,
            recv_sem=recv_sem.at[block],
            device_id={"feat": target},
            device_id_type=MESH,
        )

    all_ref[me] = cot_ref[...].astype(jnp.bfloat16)

    barrier = pltpu.get_barrier_semaphore()
    pl.semaphore_signal(barrier, inc=1, device_id={"feat": mate}, device_id_type=MESH)

    @pl.when(z + 1 < deep)
    def _():
        pl.semaphore_signal(barrier, inc=1, device_id={"feat": me + 2}, device_id_type=MESH)

    @pl.when(z > 0)
    def _():
        pl.semaphore_signal(barrier, inc=1, device_id={"feat": me - 2}, device_id_type=MESH)

    pl.semaphore_wait(barrier, 1 + jnp.where(z + 1 < deep, 1, 0) + jnp.where(z > 0, 1, 0))

    to(me, side_sem.at[z], mate).start()

    @pl.when(z + 1 < deep)
    def _():
        to(me, up_sem.at[z], me + 2).start()

    @pl.when(z > 0)
    def _():
        to(me, down_sem.at[z], me - 2).start()

    for step in range(1, deep):
        low, high = z - step, z + step

        @pl.when(low >= 0)
        def _():
            block = 2 * low + y
            to(block, side_sem.at[low], mate).wait_recv()

            @pl.when(z + 1 < deep)
            def _():
                to(block, up_sem.at[low], me + 2).start()

            to(block, side_sem.at[low], mate).start()

        @pl.when(high < deep)
        def _():
            block = 2 * high + y
            to(block, side_sem.at[high], mate).wait_recv()

            @pl.when(z > 0)
            def _():
                to(block, down_sem.at[high], me - 2).start()

            to(block, side_sem.at[high], mate).start()

    for row in range(deep):
        to(2 * row + 1 - y, side_sem.at[row], mate).wait_recv()
    for row in range(deep):
        block = 2 * row + y
        to(block, side_sem.at[row], mate).wait_send()

        @pl.when((row <= z) & (z + 1 < deep))
        def _():
            to(block, up_sem.at[row], mate).wait_send()

        @pl.when((row >= z) & (z > 0))
        def _():
            to(block, down_sem.at[row], mate).wait_send()


def gather(cot, n):
    tok, width = cot.shape
    deep = n // 2
    return pl.pallas_call(
        functools.partial(gather_kernel, n),
        out_shape=jax.ShapeDtypeStruct((n, tok, width), jnp.bfloat16),
        in_specs=[pl.BlockSpec(memory_space=pltpu.VMEM)],
        out_specs=pl.BlockSpec(memory_space=pltpu.VMEM),
        scratch_shapes=[
            pltpu.SemaphoreType.DMA((deep,)),
            pltpu.SemaphoreType.DMA((deep,)),
            pltpu.SemaphoreType.DMA((deep,)),
            pltpu.SemaphoreType.DMA((n,)),
        ],
        compiler_params=pltpu.CompilerParams(
            collective_id=0, has_side_effects=True, vmem_limit_bytes=24 * 1024 * 1024
        ),
        cost_estimate=pl.CostEstimate(
            flops=0, bytes_accessed=40 * n * tok * width, transcendentals=0
        ),
    )(cot)


def body(inputs, preacts, cotangent, w_enc, w_dec):
    n = lax.axis_size("feat")
    deep = n // 2
    tok = inputs.shape[0]
    f_loc = preacts.shape[1]
    me = lax.axis_index("feat")
    z, y = me // 2, lax.rem(me, 2)
    tgt_index = lax.axis_index("tgt")
    half_width = inputs.shape[1] // lax.axis_size("tgt")

    back_all = gather(cotangent[0], n)
    input_half = lax.dynamic_slice_in_dim(inputs, tgt_index * half_width, half_width, 1).astype(
        jnp.bfloat16
    )
    back_all, input_half = lax.optimization_barrier((back_all, input_half))
    line = jnp.zeros((deep, tok, half_width), jnp.bfloat16)
    line = lax.dynamic_update_index_in_dim(line, input_half, z, 0)
    for step in range(1, deep):
        got = lax.ppermute(input_half, "feat", [(i, (i + 2 * step) % n) for i in range(n)])
        line = lax.dynamic_update_index_in_dim(line, got, lax.rem(z + deep - step, deep), 0)
    back_all = back_all.reshape(n * tok, -1)

    partial_value = lax.dot_general(
        back_all, w_dec[0], (((1,), (1,)), ((), ())), preferred_element_type=jnp.float32
    ).astype(jnp.bfloat16)
    other = lax.ppermute(partial_value, "tgt", [(0, 1), (1, 0)])
    other, line = lax.optimization_barrier((other, line))
    mates = lax.ppermute(line, "feat", [(i, i ^ 1) for i in range(n)])
    summed = partial_value.astype(jnp.float32) + other.astype(jnp.float32)
    pre_grad = jnp.where(preacts > 0, summed, jnp.zeros_like(summed)).astype(jnp.bfloat16)
    grad_bias = jnp.sum(pre_grad.astype(jnp.float32), axis=0)

    enc_half = lax.dynamic_slice_in_dim(w_enc, tgt_index * half_width, half_width, 0)
    part = lax.dot_general(
        pre_grad, enc_half, (((1,), (1,)), ((), ())), preferred_element_type=jnp.float32
    ).astype(jnp.bfloat16)
    part = part.reshape(deep, 2, tok, half_width)
    theirs = lax.dynamic_index_in_dim(part, 1 - y, 1, keepdims=False)
    mine = lax.dynamic_index_in_dim(part, y, 1, keepdims=False)
    arrived = lax.ppermute(theirs, "feat", [(i, i ^ 1) for i in range(n)])

    active = jnp.maximum(preacts, 0)
    grad_dec = lax.dot_general(
        active, back_all, (((0,), (0,)), ((), ())), preferred_element_type=jnp.float32
    )[None]

    both = mine.astype(jnp.float32) + arrived.astype(jnp.float32)
    total = lax.dynamic_index_in_dim(both, z, 0, keepdims=False)
    sent = both.astype(jnp.bfloat16)
    for step in range(1, deep):
        block = lax.dynamic_index_in_dim(sent, lax.rem(z + step, deep), 0, keepdims=False)
        got = lax.ppermute(block, "feat", [(i, (i + 2 * step) % n) for i in range(n)])
        total = total + got.astype(jnp.float32)
    input_all = jnp.stack(
        [jnp.where(y == 0, line, mates), jnp.where(y == 0, mates, line)], axis=1
    ).reshape(n * tok, half_width)
    grad_enc = lax.dot_general(
        input_all, pre_grad, (((0,), (0,)), ((), ())), preferred_element_type=jnp.float32
    )
    return (grad_dec, grad_enc, grad_bias, total)


def solution(mesh):
    in_specs = (
        P(("groups", "feat"), None),
        P("groups", "feat"),
        P("tgt", ("groups", "feat"), None),
        P(None, "feat"),
        P("tgt", "feat", None),
    )
    out_specs = (
        P(("groups", "tgt"), "feat", None),
        P(("groups", "tgt"), "feat"),
        P(("groups", "feat")),
        P(("groups", "feat"), "tgt"),
    )
    return jax.shard_map(body, mesh=mesh, in_specs=in_specs, out_specs=out_specs, check_vma=False)
```

```python
import functools

import jax
import jax.numpy as jnp
from jax import lax
from jax.experimental import pallas as pl
from jax.experimental.pallas import tpu as pltpu
from jax.sharding import PartitionSpec as P

MESH = pl.DeviceIdType.MESH


def gather_kernel(
    n,
    cot_ref, half_ref, dec_ref,
    all_ref, line_ref, part_ref, other_ref,
    dec, dec_sem, up_sem, down_sem, side_sem, recv_sem,
    line_up, line_down, line_recv, swap_send, swap_recv,
):
    deep = n // 2
    tok, width = cot_ref.shape
    f_loc = dec_ref.shape[0]
    tile = min(512, f_loc)
    me = lax.axis_index("feat")
    core = lax.axis_index("tgt")
    z, y = me // 2, lax.rem(me, 2)
    mate = 2 * z + 1 - y
    above, below = z + 1 < deep, z > 0

    def to(block, sem, target):
        return pltpu.make_async_remote_copy(
            src_ref=all_ref.at[block],
            dst_ref=all_ref.at[block],
            send_sem=sem,
            recv_sem=recv_sem.at[block],
            device_id={"feat": target},
            device_id_type=MESH,
        )

    def line_to(row, sem, target):
        return pltpu.make_async_remote_copy(
            src_ref=line_ref.at[row],
            dst_ref=line_ref.at[row],
            send_sem=sem,
            recv_sem=line_recv.at[row],
            device_id={"feat": target},
            device_id_type=MESH,
        )

    def swap(row):
        return pltpu.make_async_remote_copy(
            src_ref=part_ref.at[row],
            dst_ref=other_ref.at[row],
            send_sem=swap_send.at[row],
            recv_sem=swap_recv.at[row],
            device_id={"tgt": 1 - core},
            device_id_type=MESH,
        )

    fetch = pltpu.make_async_copy(dec_ref, dec, dec_sem)
    fetch.start()
    all_ref[me] = cot_ref[...].astype(jnp.bfloat16)
    line_ref[z] = half_ref[...]

    barrier = pltpu.get_barrier_semaphore()
    pl.semaphore_signal(barrier, inc=1, device_id={"feat": mate}, device_id_type=MESH)
    pl.semaphore_signal(barrier, inc=1, device_id={"tgt": 1 - core}, device_id_type=MESH)

    @pl.when(above)
    def _():
        pl.semaphore_signal(barrier, inc=1, device_id={"feat": me + 2}, device_id_type=MESH)

    @pl.when(below)
    def _():
        pl.semaphore_signal(barrier, inc=1, device_id={"feat": me - 2}, device_id_type=MESH)

    pl.semaphore_wait(barrier, 2 + jnp.where(above, 1, 0) + jnp.where(below, 1, 0))

    def place(step):
        away = (step + 1) // 2
        return z + jnp.where(lax.rem(step, 2) == 1, -away, away)

    lag = 3

    @pl.loop(0, 2 * deep - 1 + lag)
    def _(step):
        row = place(step)

        @pl.when((row >= 0) & (row < deep) & (step < 2 * deep - 1))
        def _():
            block = 2 * row + y

            @pl.when(step > 0)
            def _():
                to(block, side_sem.at[row], mate).wait_recv()

            to(block, side_sem.at[row], mate).start()

            @pl.when((row <= z) & above)
            def _():
                to(block, up_sem.at[row], me + 2).start()

            @pl.when((row >= z) & below)
            def _():
                to(block, down_sem.at[row], me - 2).start()

        @pl.when(step == lag)
        def _():
            fetch.wait()

        late = step - lag
        old = place(jnp.maximum(late, 0))

        @pl.when((late >= 0) & (old >= 0) & (old < deep))
        def _():
            @pl.when(late > 0)
            def _():
                line_to(old, line_up.at[old], mate).wait_recv()

            @pl.when((old <= z) & above)
            def _():
                line_to(old, line_up.at[old], me + 2).start()

            @pl.when((old >= z) & below)
            def _():
                line_to(old, line_down.at[old], me - 2).start()

            to(2 * old + 1 - y, side_sem.at[old], mate).wait_recv()
            rows = all_ref[pl.ds(2 * old, 2)].reshape(2 * tok, width)

            @pl.loop(0, f_loc // tile)
            def _(t):
                span = pl.ds(pl.multiple_of(t * tile, tile), tile)
                part_ref[old, :, span] = lax.dot_general(
                    rows, dec[span, :], (((1,), (1,)), ((), ())),
                    preferred_element_type=jnp.float32,
                ).astype(jnp.bfloat16)

            swap(old).start()

    for row in range(deep):
        block = 2 * row + y
        swap(row).wait()
        to(block, side_sem.at[row], mate).wait_send()

        @pl.when((row <= z) & above)
        def _():
            to(block, up_sem.at[row], mate).wait_send()
            line_to(row, line_up.at[row], mate).wait_send()

        @pl.when((row >= z) & below)
        def _():
            to(block, down_sem.at[row], mate).wait_send()
            line_to(row, line_down.at[row], mate).wait_send()


def gather(cot, half, dec, n):
    tok, width = cot.shape
    f_loc = dec.shape[0]
    deep = n // 2
    vmem = pl.BlockSpec(memory_space=pltpu.VMEM)
    chains = [pltpu.SemaphoreType.DMA((deep,))] * 3
    return pl.pallas_call(
        functools.partial(gather_kernel, n),
        out_shape=(
            jax.ShapeDtypeStruct((n, tok, width), jnp.bfloat16),
            jax.ShapeDtypeStruct((deep,) + half.shape, jnp.bfloat16),
            jax.ShapeDtypeStruct((deep, 2 * tok, f_loc), jnp.bfloat16),
            jax.ShapeDtypeStruct((deep, 2 * tok, f_loc), jnp.bfloat16),
        ),
        in_specs=[vmem, vmem, pl.BlockSpec(memory_space=pl.ANY)],
        out_specs=(vmem, vmem, vmem, vmem),
        scratch_shapes=[
            pltpu.VMEM(dec.shape, jnp.bfloat16),
            pltpu.SemaphoreType.DMA,
            *chains,
            pltpu.SemaphoreType.DMA((n,)),
            *chains,
            pltpu.SemaphoreType.DMA((deep,)),
            pltpu.SemaphoreType.DMA((deep,)),
        ],
        compiler_params=pltpu.CompilerParams(
            collective_id=0, has_side_effects=True, vmem_limit_bytes=40 * 1024 * 1024
        ),
        cost_estimate=pl.CostEstimate(
            flops=2 * n * tok * width * f_loc,
            bytes_accessed=40 * n * tok * width,
            transcendentals=0,
        ),
    )(cot, half, dec)


def body(inputs, preacts, cotangent, w_enc, w_dec):
    n = lax.axis_size("feat")
    deep = n // 2
    tok = inputs.shape[0]
    f_loc = preacts.shape[1]
    me = lax.axis_index("feat")
    z, y = me // 2, lax.rem(me, 2)
    tgt_index = lax.axis_index("tgt")
    half_width = inputs.shape[1] // lax.axis_size("tgt")

    input_half = lax.dynamic_slice_in_dim(inputs, tgt_index * half_width, half_width, 1).astype(
        jnp.bfloat16
    )
    back_all, line, partial_value, other = gather(cotangent[0], input_half, w_dec[0], n)
    mates = lax.ppermute(line, "feat", [(i, i ^ 1) for i in range(n)])
    back_all = back_all.reshape(n * tok, -1)
    partial_value = partial_value.reshape(n * tok, f_loc)
    other = other.reshape(n * tok, f_loc)
    summed = partial_value.astype(jnp.float32) + other.astype(jnp.float32)
    pre_grad = jnp.where(preacts > 0, summed, jnp.zeros_like(summed)).astype(jnp.bfloat16)
    grad_bias = jnp.sum(pre_grad.astype(jnp.float32), axis=0)

    enc_half = lax.dynamic_slice_in_dim(w_enc, tgt_index * half_width, half_width, 0)
    part = lax.dot_general(
        pre_grad, enc_half, (((1,), (1,)), ((), ())), preferred_element_type=jnp.float32
    ).astype(jnp.bfloat16)
    part = part.reshape(deep, 2, tok, half_width)
    theirs = lax.dynamic_index_in_dim(part, 1 - y, 1, keepdims=False)
    mine = lax.dynamic_index_in_dim(part, y, 1, keepdims=False)
    arrived = lax.ppermute(theirs, "feat", [(i, i ^ 1) for i in range(n)])

    active = jnp.maximum(preacts, 0)
    grad_dec = lax.dot_general(
        active, back_all, (((0,), (0,)), ((), ())), preferred_element_type=jnp.float32
    )[None]

    both = mine.astype(jnp.float32) + arrived.astype(jnp.float32)
    total = lax.dynamic_index_in_dim(both, z, 0, keepdims=False)
    sent = both.astype(jnp.bfloat16)
    for step in range(1, deep):
        block = lax.dynamic_index_in_dim(sent, lax.rem(z + step, deep), 0, keepdims=False)
        got = lax.ppermute(block, "feat", [(i, (i + 2 * step) % n) for i in range(n)])
        total = total + got.astype(jnp.float32)
    input_all = jnp.stack(
        [jnp.where(y == 0, line, mates), jnp.where(y == 0, mates, line)], axis=1
    ).reshape(n * tok, half_width)
    grad_enc = lax.dot_general(
        input_all, pre_grad, (((0,), (0,)), ((), ())), preferred_element_type=jnp.float32
    )
    return (grad_dec, grad_enc, grad_bias, total)


def solution(mesh):
    in_specs = (
        P(("groups", "feat"), None),
        P("groups", "feat"),
        P("tgt", ("groups", "feat"), None),
        P(None, "feat"),
        P("tgt", "feat", None),
    )
    out_specs = (
        P(("groups", "tgt"), "feat", None),
        P(("groups", "tgt"), "feat"),
        P(("groups", "feat")),
        P(("groups", "feat"), "tgt"),
    )
    return jax.shard_map(body, mesh=mesh, in_specs=in_specs, out_specs=out_specs, check_vma=False)
```

```python
import functools

import jax
import jax.numpy as jnp
from jax import lax
from jax.experimental import pallas as pl
from jax.experimental.pallas import tpu as pltpu
from jax.sharding import PartitionSpec as P

MESH = pl.DeviceIdType.MESH


def gather_kernel(
    n,
    cot_ref, half_ref, dec_ref,
    all_ref, line_ref, part_ref, other_ref,
    dec, dec_sem, up_sem, down_sem, side_sem, recv_sem,
    line_up, line_down, line_recv, swap_send, swap_recv,
):
    deep = n // 2
    tok, width = cot_ref.shape
    f_loc = dec_ref.shape[0]
    tile = min(512, f_loc)
    me = lax.axis_index("feat")
    core = lax.axis_index("tgt")
    z, y = me // 2, lax.rem(me, 2)
    mate = 2 * z + 1 - y
    above, below = z + 1 < deep, z > 0

    def to(block, sem, target):
        return pltpu.make_async_remote_copy(
            src_ref=all_ref.at[block],
            dst_ref=all_ref.at[block],
            send_sem=sem,
            recv_sem=recv_sem.at[block],
            device_id={"feat": target},
            device_id_type=MESH,
        )

    def line_to(row, sem, target):
        return pltpu.make_async_remote_copy(
            src_ref=line_ref.at[row],
            dst_ref=line_ref.at[row],
            send_sem=sem,
            recv_sem=line_recv.at[row],
            device_id={"feat": target},
            device_id_type=MESH,
        )

    def swap(row):
        return pltpu.make_async_remote_copy(
            src_ref=part_ref.at[row],
            dst_ref=other_ref.at[row],
            send_sem=swap_send.at[row],
            recv_sem=swap_recv.at[row],
            device_id={"tgt": 1 - core},
            device_id_type=MESH,
        )

    fetch = pltpu.make_async_copy(dec_ref, dec, dec_sem)
    fetch.start()
    all_ref[me] = cot_ref[...].astype(jnp.bfloat16)
    line_ref[z] = half_ref[...]

    barrier = pltpu.get_barrier_semaphore()
    pl.semaphore_signal(barrier, inc=1, device_id={"feat": mate}, device_id_type=MESH)
    pl.semaphore_signal(barrier, inc=1, device_id={"tgt": 1 - core}, device_id_type=MESH)

    @pl.when(above)
    def _():
        pl.semaphore_signal(barrier, inc=1, device_id={"feat": me + 2}, device_id_type=MESH)

    @pl.when(below)
    def _():
        pl.semaphore_signal(barrier, inc=1, device_id={"feat": me - 2}, device_id_type=MESH)

    pl.semaphore_wait(barrier, 2 + jnp.where(above, 1, 0) + jnp.where(below, 1, 0))

    def place(step):
        away = (step + 1) // 2
        return z + jnp.where(lax.rem(step, 2) == 1, -away, away)

    lag = 3

    @pl.loop(0, 2 * deep - 1 + lag)
    def _(step):
        row = place(step)

        @pl.when((row >= 0) & (row < deep) & (step < 2 * deep - 1))
        def _():
            block = 2 * row + y

            @pl.when(step > 0)
            def _():
                to(block, side_sem.at[row], mate).wait_recv()

            to(block, side_sem.at[row], mate).start()

            @pl.when((row <= z) & above)
            def _():
                to(block, up_sem.at[row], me + 2).start()

            @pl.when((row >= z) & below)
            def _():
                to(block, down_sem.at[row], me - 2).start()

        @pl.when(step == lag)
        def _():
            fetch.wait()

        late = step - lag
        old = place(jnp.maximum(late, 0))

        @pl.when((late >= 0) & (old >= 0) & (old < deep))
        def _():
            @pl.when(late > 0)
            def _():
                line_to(old, line_up.at[old], mate).wait_recv()

            @pl.when((old <= z) & above)
            def _():
                line_to(old, line_up.at[old], me + 2).start()

            @pl.when((old >= z) & below)
            def _():
                line_to(old, line_down.at[old], me - 2).start()

            to(2 * old + 1 - y, side_sem.at[old], mate).wait_recv()
            rows = all_ref[pl.ds(2 * old, 2)].reshape(2 * tok, width)

            @pl.loop(0, f_loc // tile)
            def _(t):
                span = pl.ds(pl.multiple_of(t * tile, tile), tile)
                part_ref[old, :, span] = lax.dot_general(
                    rows, dec[span, :], (((1,), (1,)), ((), ())),
                    preferred_element_type=jnp.float32,
                ).astype(jnp.bfloat16)

            swap(old).start()

    for row in range(deep):
        block = 2 * row + y
        swap(row).wait()
        to(block, side_sem.at[row], mate).wait_send()

        @pl.when((row <= z) & above)
        def _():
            to(block, up_sem.at[row], mate).wait_send()
            line_to(row, line_up.at[row], mate).wait_send()

        @pl.when((row >= z) & below)
        def _():
            to(block, down_sem.at[row], mate).wait_send()
            line_to(row, line_down.at[row], mate).wait_send()


def gather(cot, half, dec, n):
    tok, width = cot.shape
    f_loc = dec.shape[0]
    deep = n // 2
    vmem = pl.BlockSpec(memory_space=pltpu.VMEM)
    chains = [pltpu.SemaphoreType.DMA((deep,))] * 3
    return pl.pallas_call(
        functools.partial(gather_kernel, n),
        out_shape=(
            jax.ShapeDtypeStruct((n, tok, width), jnp.bfloat16),
            jax.ShapeDtypeStruct((deep,) + half.shape, jnp.bfloat16),
            jax.ShapeDtypeStruct((deep, 2 * tok, f_loc), jnp.bfloat16),
            jax.ShapeDtypeStruct((deep, 2 * tok, f_loc), jnp.bfloat16),
        ),
        in_specs=[vmem, vmem, pl.BlockSpec(memory_space=pl.ANY)],
        out_specs=(vmem, vmem, vmem, vmem),
        scratch_shapes=[
            pltpu.VMEM(dec.shape, jnp.bfloat16),
            pltpu.SemaphoreType.DMA,
            *chains,
            pltpu.SemaphoreType.DMA((n,)),
            *chains,
            pltpu.SemaphoreType.DMA((deep,)),
            pltpu.SemaphoreType.DMA((deep,)),
        ],
        compiler_params=pltpu.CompilerParams(
            collective_id=0, has_side_effects=True, vmem_limit_bytes=40 * 1024 * 1024
        ),
        cost_estimate=pl.CostEstimate(
            flops=2 * n * tok * width * f_loc,
            bytes_accessed=40 * n * tok * width,
            transcendentals=0,
        ),
    )(cot, half, dec)


def body(inputs, preacts, cotangent, w_enc, w_dec):
    n = lax.axis_size("feat")
    deep = n // 2
    tok = inputs.shape[0]
    f_loc = preacts.shape[1]
    me = lax.axis_index("feat")
    z, y = me // 2, lax.rem(me, 2)
    tgt_index = lax.axis_index("tgt")
    half_width = inputs.shape[1] // lax.axis_size("tgt")

    input_half = lax.dynamic_slice_in_dim(inputs, tgt_index * half_width, half_width, 1).astype(
        jnp.bfloat16
    )
    back_all, line, partial_value, other = gather(cotangent[0], input_half, w_dec[0], n)
    mates = lax.ppermute(line, "feat", [(i, i ^ 1) for i in range(n)])
    back_all = back_all.reshape(n * tok, -1)
    partial_value = partial_value.reshape(n * tok, f_loc)
    other = other.reshape(n * tok, f_loc)
    summed = partial_value.astype(jnp.float32) + other.astype(jnp.float32)
    pre_grad = jnp.where(preacts > 0, summed, jnp.zeros_like(summed)).astype(jnp.bfloat16)
    grad_bias = jnp.sum(pre_grad.astype(jnp.float32), axis=0)

    enc_half = lax.dynamic_slice_in_dim(w_enc, tgt_index * half_width, half_width, 0)
    part = lax.dot_general(
        pre_grad, enc_half, (((1,), (1,)), ((), ())), preferred_element_type=jnp.float32
    ).astype(jnp.bfloat16)
    part = part.reshape(deep, 2, tok, half_width)
    cut = half_width - (half_width * 4 // 9) // 128 * 128
    across = [(i, i ^ 1) for i in range(n)]
    along = [[(i, (i + 2 * step) % n) for i in range(n)] for step in range(deep)]
    first, second = part[..., :cut], part[..., cut:]
    theirs = lax.dynamic_index_in_dim(first, 1 - y, 1, keepdims=False)
    mine = lax.dynamic_index_in_dim(first, y, 1, keepdims=False)
    arrived = lax.ppermute(theirs, "feat", across)
    pairs = [
        lax.ppermute(
            lax.dynamic_index_in_dim(second, lax.rem(z + step, deep), 0, keepdims=False),
            "feat", along[step],
        )
        for step in range(1, deep)
    ]

    active = jnp.maximum(preacts, 0)
    grad_dec = lax.dot_general(
        active, back_all, (((0,), (0,)), ((), ())), preferred_element_type=jnp.float32
    )[None]

    both = mine.astype(jnp.float32) + arrived.astype(jnp.float32)
    pair = lax.dynamic_index_in_dim(second, z, 0, keepdims=False).astype(jnp.float32)
    for got in pairs:
        pair = pair + got.astype(jnp.float32)
    sent = both.astype(jnp.bfloat16)
    rest = lax.ppermute(
        lax.dynamic_index_in_dim(pair, 1 - y, 0, keepdims=False).astype(jnp.bfloat16),
        "feat", across,
    )
    blocks = [
        lax.ppermute(
            lax.dynamic_index_in_dim(sent, lax.rem(z + step, deep), 0, keepdims=False),
            "feat", along[step],
        )
        for step in range(1, deep)
    ]
    input_all = jnp.stack(
        [jnp.where(y == 0, line, mates), jnp.where(y == 0, mates, line)], axis=1
    ).reshape(n * tok, half_width)
    grad_enc = lax.dot_general(
        input_all, pre_grad, (((0,), (0,)), ((), ())), preferred_element_type=jnp.float32
    )
    grad_enc, rest, blocks = lax.optimization_barrier((grad_enc, rest, blocks))
    total = lax.dynamic_index_in_dim(both, z, 0, keepdims=False)
    for block in blocks:
        total = total + block.astype(jnp.float32)
    rest = lax.dynamic_index_in_dim(pair, y, 0, keepdims=False) + rest.astype(jnp.float32)
    total = jnp.concatenate([total, rest], axis=1)
    return (grad_dec, grad_enc, grad_bias, total)


def solution(mesh):
    in_specs = (
        P(("groups", "feat"), None),
        P("groups", "feat"),
        P("tgt", ("groups", "feat"), None),
        P(None, "feat"),
        P("tgt", "feat", None),
    )
    out_specs = (
        P(("groups", "tgt"), "feat", None),
        P(("groups", "tgt"), "feat"),
        P(("groups", "feat")),
        P(("groups", "feat"), "tgt"),
    )
    return jax.shard_map(body, mesh=mesh, in_specs=in_specs, out_specs=out_specs, check_vma=False)
```

```python
import functools

import jax
import jax.numpy as jnp
from jax import lax
from jax.experimental import pallas as pl
from jax.experimental.pallas import tpu as pltpu
from jax.sharding import PartitionSpec as P

MESH = pl.DeviceIdType.MESH


def gather_kernel(
    n,
    cot_ref, half_ref, dec_ref,
    all_ref, line_ref, part_ref, other_ref,
    dec, dec_sem, up_sem, down_sem, side_sem, recv_sem,
    line_up, line_down, line_recv, swap_send, swap_recv,
):
    deep = n // 2
    tok, width = cot_ref.shape
    f_loc = dec_ref.shape[0]
    tile = min(512, f_loc)
    me = lax.axis_index("feat")
    core = lax.axis_index("tgt")
    z, y = me // 2, lax.rem(me, 2)
    mate = 2 * z + 1 - y
    above, below = z + 1 < deep, z > 0

    def to(block, sem, target):
        return pltpu.make_async_remote_copy(
            src_ref=all_ref.at[block],
            dst_ref=all_ref.at[block],
            send_sem=sem,
            recv_sem=recv_sem.at[block],
            device_id={"feat": target},
            device_id_type=MESH,
        )

    def line_to(row, sem, target):
        return pltpu.make_async_remote_copy(
            src_ref=line_ref.at[row],
            dst_ref=line_ref.at[row],
            send_sem=sem,
            recv_sem=line_recv.at[row],
            device_id={"feat": target},
            device_id_type=MESH,
        )

    def swap(row):
        return pltpu.make_async_remote_copy(
            src_ref=part_ref.at[row],
            dst_ref=other_ref.at[row],
            send_sem=swap_send.at[row],
            recv_sem=swap_recv.at[row],
            device_id={"tgt": 1 - core},
            device_id_type=MESH,
        )

    fetch = pltpu.make_async_copy(dec_ref, dec, dec_sem)
    fetch.start()
    all_ref[me] = cot_ref[...].astype(jnp.bfloat16)
    line_ref[z] = half_ref[...]

    barrier = pltpu.get_barrier_semaphore()
    pl.semaphore_signal(barrier, inc=1, device_id={"feat": mate}, device_id_type=MESH)
    pl.semaphore_signal(barrier, inc=1, device_id={"tgt": 1 - core}, device_id_type=MESH)

    @pl.when(above)
    def _():
        pl.semaphore_signal(barrier, inc=1, device_id={"feat": me + 2}, device_id_type=MESH)

    @pl.when(below)
    def _():
        pl.semaphore_signal(barrier, inc=1, device_id={"feat": me - 2}, device_id_type=MESH)

    pl.semaphore_wait(barrier, 2 + jnp.where(above, 1, 0) + jnp.where(below, 1, 0))

    def place(step):
        away = (step + 1) // 2
        return z + jnp.where(lax.rem(step, 2) == 1, -away, away)

    lag = 3

    @pl.loop(0, 2 * deep - 1 + lag)
    def _(step):
        row = place(step)

        @pl.when((row >= 0) & (row < deep) & (step < 2 * deep - 1))
        def _():
            block = 2 * row + y

            @pl.when(step > 0)
            def _():
                to(block, side_sem.at[row], mate).wait_recv()

            to(block, side_sem.at[row], mate).start()

            @pl.when((row <= z) & above)
            def _():
                to(block, up_sem.at[row], me + 2).start()

            @pl.when((row >= z) & below)
            def _():
                to(block, down_sem.at[row], me - 2).start()

        @pl.when(step == lag)
        def _():
            fetch.wait()

        late = step - lag
        old = place(jnp.maximum(late, 0))

        @pl.when((late >= 0) & (old >= 0) & (old < deep))
        def _():
            @pl.when(late > 0)
            def _():
                line_to(old, line_up.at[old], mate).wait_recv()

            @pl.when((old <= z) & above)
            def _():
                line_to(old, line_up.at[old], me + 2).start()

            @pl.when((old >= z) & below)
            def _():
                line_to(old, line_down.at[old], me - 2).start()

            to(2 * old + 1 - y, side_sem.at[old], mate).wait_recv()
            rows = all_ref[pl.ds(2 * old, 2)].reshape(2 * tok, width)

            @pl.loop(0, f_loc // tile)
            def _(t):
                span = pl.ds(pl.multiple_of(t * tile, tile), tile)
                part_ref[old, :, span] = lax.dot_general(
                    rows, dec[span, :], (((1,), (1,)), ((), ())),
                    preferred_element_type=jnp.float32,
                ).astype(jnp.bfloat16)

            swap(old).start()

    for row in range(deep):
        block = 2 * row + y
        swap(row).wait()
        to(block, side_sem.at[row], mate).wait_send()

        @pl.when((row <= z) & above)
        def _():
            to(block, up_sem.at[row], mate).wait_send()
            line_to(row, line_up.at[row], mate).wait_send()

        @pl.when((row >= z) & below)
        def _():
            to(block, down_sem.at[row], mate).wait_send()
            line_to(row, line_down.at[row], mate).wait_send()


def gather(cot, half, dec, n):
    tok, width = cot.shape
    f_loc = dec.shape[0]
    deep = n // 2
    vmem = pl.BlockSpec(memory_space=pltpu.VMEM)
    chains = [pltpu.SemaphoreType.DMA((deep,))] * 3
    return pl.pallas_call(
        functools.partial(gather_kernel, n),
        out_shape=(
            jax.ShapeDtypeStruct((n, tok, width), jnp.bfloat16),
            jax.ShapeDtypeStruct((deep,) + half.shape, jnp.bfloat16),
            jax.ShapeDtypeStruct((deep, 2 * tok, f_loc), jnp.bfloat16),
            jax.ShapeDtypeStruct((deep, 2 * tok, f_loc), jnp.bfloat16),
        ),
        in_specs=[vmem, vmem, pl.BlockSpec(memory_space=pl.ANY)],
        out_specs=(vmem, vmem, vmem, vmem),
        scratch_shapes=[
            pltpu.VMEM(dec.shape, jnp.bfloat16),
            pltpu.SemaphoreType.DMA,
            *chains,
            pltpu.SemaphoreType.DMA((n,)),
            *chains,
            pltpu.SemaphoreType.DMA((deep,)),
            pltpu.SemaphoreType.DMA((deep,)),
        ],
        compiler_params=pltpu.CompilerParams(
            collective_id=0, has_side_effects=True, vmem_limit_bytes=40 * 1024 * 1024
        ),
        cost_estimate=pl.CostEstimate(
            flops=2 * n * tok * width * f_loc,
            bytes_accessed=40 * n * tok * width,
            transcendentals=0,
        ),
    )(cot, half, dec)


def body(inputs, preacts, cotangent, w_enc, w_dec):
    n = lax.axis_size("feat")
    deep = n // 2
    tok = inputs.shape[0]
    f_loc = preacts.shape[1]
    me = lax.axis_index("feat")
    z, y = me // 2, lax.rem(me, 2)
    tgt_index = lax.axis_index("tgt")
    half_width = inputs.shape[1] // lax.axis_size("tgt")

    input_half = lax.dynamic_slice_in_dim(inputs, tgt_index * half_width, half_width, 1).astype(
        jnp.bfloat16
    )
    back_all, line, partial_value, other = gather(cotangent[0], input_half, w_dec[0], n)
    mates = lax.ppermute(line, "feat", [(i, i ^ 1) for i in range(n)])
    back_all = back_all.reshape(n * tok, -1)
    partial_value = partial_value.reshape(n * tok, f_loc)
    other = other.reshape(n * tok, f_loc)
    summed = partial_value.astype(jnp.float32) + other.astype(jnp.float32)
    pre_grad = jnp.where(preacts > 0, summed, jnp.zeros_like(summed)).astype(jnp.bfloat16)
    grad_bias = jnp.sum(pre_grad.astype(jnp.float32), axis=0)

    cut = half_width - (half_width * 4 // 9) // 128 * 128
    across = [(i, i ^ 1) for i in range(n)]
    along = [[(i, (i + 2 * step) % n) for i in range(n)] for step in range(deep)]

    def columns(start, size):
        enc_part = lax.dynamic_slice_in_dim(w_enc, tgt_index * half_width + start, size, 0)
        return lax.dot_general(
            pre_grad, enc_part, (((1,), (1,)), ((), ())), preferred_element_type=jnp.float32
        ).astype(jnp.bfloat16).reshape(deep, 2, tok, size)

    first, second = columns(0, cut), columns(cut, half_width - cut)
    theirs = lax.dynamic_index_in_dim(first, 1 - y, 1, keepdims=False)
    mine = lax.dynamic_index_in_dim(first, y, 1, keepdims=False)
    arrived = lax.ppermute(theirs, "feat", across)
    pairs = [
        lax.ppermute(
            lax.dynamic_index_in_dim(second, lax.rem(z + step, deep), 0, keepdims=False),
            "feat", along[step],
        )
        for step in range(1, deep)
    ]

    active = jnp.maximum(preacts, 0)
    grad_dec = lax.dot_general(
        active, back_all, (((0,), (0,)), ((), ())), preferred_element_type=jnp.float32
    )[None]

    both = mine.astype(jnp.float32) + arrived.astype(jnp.float32)
    pair = lax.dynamic_index_in_dim(second, z, 0, keepdims=False).astype(jnp.float32)
    for got in pairs:
        pair = pair + got.astype(jnp.float32)
    sent = both.astype(jnp.bfloat16)
    rest = lax.ppermute(
        lax.dynamic_index_in_dim(pair, 1 - y, 0, keepdims=False).astype(jnp.bfloat16),
        "feat", across,
    )
    blocks = [
        lax.ppermute(
            lax.dynamic_index_in_dim(sent, lax.rem(z + step, deep), 0, keepdims=False),
            "feat", along[step],
        )
        for step in range(1, deep)
    ]
    input_all = jnp.stack(
        [jnp.where(y == 0, line, mates), jnp.where(y == 0, mates, line)], axis=1
    ).reshape(n * tok, half_width)
    grad_enc = lax.dot_general(
        input_all, pre_grad, (((0,), (0,)), ((), ())), preferred_element_type=jnp.float32
    )
    grad_enc, rest, blocks = lax.optimization_barrier((grad_enc, rest, blocks))
    total = lax.dynamic_index_in_dim(both, z, 0, keepdims=False)
    for block in blocks:
        total = total + block.astype(jnp.float32)
    rest = lax.dynamic_index_in_dim(pair, y, 0, keepdims=False) + rest.astype(jnp.float32)
    total = jnp.concatenate([total, rest], axis=1)
    return (grad_dec, grad_enc, grad_bias, total)


def solution(mesh):
    in_specs = (
        P(("groups", "feat"), None),
        P("groups", "feat"),
        P("tgt", ("groups", "feat"), None),
        P(None, "feat"),
        P("tgt", "feat", None),
    )
    out_specs = (
        P(("groups", "tgt"), "feat", None),
        P(("groups", "tgt"), "feat"),
        P(("groups", "feat")),
        P(("groups", "feat"), "tgt"),
    )
    return jax.shard_map(body, mesh=mesh, in_specs=in_specs, out_specs=out_specs, check_vma=False)
```
